32 devices in a mesh: sub: 8 (over z, x), lvl: 4 (over y, core).
Axes of the slice: x: 2, y: 2, z: 4, core: 2. Of those that a mesh axis runs over, the one named last changes fastest.
Arguments:
- vectors: bfloat16 [1024, 2, 256], P(('sub', 'lvl')), may hold values from -6 to 6
- self_blocks: bfloat16 [1024, 256, 256], P(('sub', 'lvl')), may hold values from -0.375 to 0.375
- near_blocks: bfloat16 [1024, 256, 256], P(('sub', 'lvl')), may hold values from -0.375 to 0.375
- near_row: int32 [1024], P(('sub', 'lvl')), may hold values from 0 to 31
- near_col: int32 [1024], P(('sub', 'lvl')), may hold values from 0 to 63
- bases: bfloat16 [1024, 256, 64], P(('sub', 'lvl')), may hold values from -0.375 to 0.375
- transfers: float32 [1984, 64, 64], P(('sub', 'lvl')), may hold values from -0.5 to 0.5
- far_row: int32 [4096], P(('sub', 'lvl')), may hold values from 0 to 31
- far_col: int32 [4096], P(('sub', 'lvl')), may hold values from 0 to 1023, as said below
- couplings: float32 [4096, 64, 64], P(('sub', 'lvl')), may hold values from -0.75 to 0.75
- root_couplings: float32 [32, 32, 64, 64], P(('sub', 'lvl')), may hold values from -1.5 to 1.5
Outputs:
- products: float32 [1024, 2, 256], P(('sub', 'lvl'))
The draws below stay inside these ranges and needn't reach their ends.
Inputs may be any that keep to these rules, and one draw needn't show every extreme that they name: `far_col`: the column leaf of an admissible pair never lies on the owning device. Of each device's 128 pairs, exactly 16 have column leaves on each of the six devices 1, 2 or 3 places before or after it (cyclically over all devices). The others lie on devices more than 3 places away, at most 16 on any one device, and exactly 16 of them on one such device.
All inputs are finite; a program needn't handle non-finite values.
Results may differ from the reference program's by a relative error of at most 0.0024.
Values may be sent and summed in bfloat16 or wider, within the bound.
No kernel may reach another device: no remote copies, remote signals or barrier semaphores. Data moves between devices by JAX's collectives and lax.ppermute only.
A program may use at most 128 MiB of HBM per device.

```python
import jax
import jax.numpy as jnp
from jax import lax

LEAF = 256
RANK = 64
LEAF_DEV = 32
NEAR_DEV = 32
FAR_DEV = 128
LEAVES = 1024
NEAR = 1024
FAR = 4096
TRANS = 1984
N_SUB = 8
N_LVL = 4


def draw_far_col(key, part):
    key = jax.random.fold_in(key, 11)
    devices = N_SUB * N_LVL
    cap = LEAF_DEV // 2
    near_deltas = jnp.repeat(jnp.array([-3, -2, -1, 1, 2, 3], jnp.int32), cap)
    far_count = devices - 7
    spread_count = LEAF_DEV - cap
    hub = jax.random.randint(jax.random.fold_in(key, 7919), (), 0, devices).astype(jnp.int32)

    def one_device(owner):
        sub_key = jax.random.fold_in(key, owner)
        first, second, third = jax.random.split(sub_key, 3)
        order = jax.random.permutation(first, far_count).astype(jnp.int32)
        hub_delta = ((hub - owner) % devices).astype(jnp.int32)
        remote = (hub_delta >= 4) & (hub_delta <= devices - 4)
        heavy = jnp.where(remote, hub_delta - 4, order[0]).astype(jnp.int32)
        slots = jnp.arange(far_count, dtype=jnp.int32)
        where_heavy = jnp.sum(jnp.where(order == heavy, slots, 0)).astype(jnp.int32)
        picks = (jnp.arange(spread_count, dtype=jnp.int32) % (far_count - 1)).astype(jnp.int32)
        picks = (picks + (picks >= where_heavy).astype(jnp.int32)).astype(jnp.int32)
        spread = order[picks]
        heavy_block = jnp.zeros((cap,), jnp.int32) + heavy
        far_deltas = (4 + jnp.concatenate([heavy_block, spread])).astype(jnp.int32)
        deltas = jnp.concatenate([near_deltas, far_deltas])
        deltas = jax.random.permutation(second, deltas).astype(jnp.int32)
        target = ((owner + deltas) % devices).astype(jnp.int32)
        within = jax.random.randint(third, (FAR_DEV,), 0, LEAF_DEV).astype(jnp.int32)
        return (target * LEAF_DEV + within).astype(jnp.int32)
    return jax.vmap(one_device)(jnp.arange(devices, dtype=jnp.int32)).reshape(FAR)


def touch_ends(result, rng, smallest, top_value):
    spot = [jax.random.randint(jax.random.fold_in(rng, axis), (), 0, length) for axis, length in enumerate(result.shape)]
    widest = result.shape.index(max(result.shape))
    beside = spot[:widest] + [(spot[widest] + 1) % result.shape[widest]] + spot[widest + 1:]
    return result.at[tuple(spot)].set(smallest).at[tuple(beside)].set(top_value)


def with_spikes(values, key, source, target, blocks, factor):
    owner, partner = [(jnp.arange(values.shape[dim]) // (values.shape[dim] // blocks)).reshape([-1 if axis == dim else 1 for axis in range(values.ndim)]) for dim in (source, target)]
    chosen = jax.random.permutation(key, blocks)[partner]
    strong = (owner == chosen) | (owner == (partner + blocks // 2) % blocks)
    return jnp.where(strong, factor * values, values)


def block_levels(rng, dims, pieces, smallest, high):
    level = 1.0
    for position, blocks in pieces:
        steps = jax.random.uniform(jax.random.fold_in(jax.random.fold_in(rng, 6), position), (blocks,), jnp.float32, smallest / len(pieces), high / len(pieces))
        level = level * jnp.repeat(jnp.exp(steps), dims[position] // blocks).reshape((-1,) + (1,) * (len(dims) - 1 - position))
    return level


def gaussian(stream_key, shape, scale, reach, cuts=(), held_as=jnp.bfloat16):
    drawn = jax.random.normal(stream_key, shape, jnp.float32) * scale
    if len(cuts) > 0:
        drawn = block_levels(stream_key, shape, cuts, -0.22, 0.18) * drawn
    return jnp.clip(drawn, min=-reach, max=reach).astype(held_as)


def heavy_noise(own_key, dims, scale, limit, shards, heavy, kind=jnp.bfloat16):
    result = scale * jax.random.normal(own_key, dims, jnp.float32)
    if shards:
        result = result * block_levels(own_key, dims, shards, -0.22, 0.18)
    return jnp.clip(with_spikes(result, jax.random.fold_in(own_key, 3), *heavy), -limit, limit).astype(kind)


def setup_inputs(seed: int = 0) -> dict:
    key_list = jax.random.split(jax.random.key(seed), 12)
    vectors = gaussian(key_list[0], (LEAVES, 2, LEAF), 1.0, 6.0, ((0, 32),))
    self_blocks = gaussian(key_list[1], (LEAVES, LEAF, LEAF), LEAF ** -0.5, 0.375, ((0, 32),))
    near_blocks = gaussian(key_list[2], (NEAR, LEAF, LEAF), LEAF ** -0.5, 0.375, ((0, 32),))
    near_row = touch_ends(jax.random.randint(key_list[3], (NEAR,), 0, LEAF_DEV), jax.random.fold_in(key_list[3], 1), 0, LEAF_DEV - 1).astype(jnp.int32)
    near_col = touch_ends(jax.random.randint(key_list[4], (NEAR,), 0, 2 * LEAF_DEV), jax.random.fold_in(key_list[4], 1), 0, (2 * LEAF_DEV) - 1).astype(jnp.int32)
    bases = gaussian(key_list[5], (LEAVES, LEAF, RANK), LEAF ** -0.5, 0.375, ((0, 32),))
    transfers = gaussian(key_list[6], (TRANS, RANK, RANK), (2 * RANK) ** -0.5, 0.5, ((0, 32),), jnp.float32)
    far_row = touch_ends(jax.random.randint(key_list[7], (FAR,), 0, LEAF_DEV), jax.random.fold_in(key_list[7], 1), 0, LEAF_DEV - 1).astype(jnp.int32)
    far_col = draw_far_col(jax.random.fold_in(key_list[11], 71), 0)
    couplings = gaussian(key_list[9], (FAR, RANK, RANK), RANK ** -0.5, 0.75, ((0, 32),), jnp.float32)
    root_couplings = heavy_noise(key_list[10], (N_SUB * N_LVL, N_SUB * N_LVL, RANK, RANK), (max(1, N_SUB * N_LVL * RANK // LEAF_DEV)) ** -0.5, 1.5, ((0, 32),), (1, 0, 32, 2.75), jnp.float32)
    return {"vectors": vectors, "self_blocks": self_blocks, "near_blocks": near_blocks, "near_row": near_row, "near_col": near_col, "bases": bases, "transfers": transfers, "far_row": far_row, "far_col": far_col, "couplings": couplings, "root_couplings": root_couplings}


HIGH = lax.Precision.HIGHEST


def tree_levels(count):
    levels = []
    offset = 0
    width = count
    while width > 1:
        levels.append((offset, width))
        offset += width
        width //= 2
    return levels


def tree_up(coeff, trans):
    for offset, width in tree_levels(coeff.shape[0]):
        prod = jnp.einsum('nvk,nkr->nvr', coeff, trans[offset:offset + width], precision=HIGH)
        coeff = prod.reshape(width // 2, 2, 2, prod.shape[-1]).sum(axis=1)
    return coeff[0]


def tree_down(top, leaf_terms, trans):
    field = top[None]
    for offset, width in reversed(tree_levels(leaf_terms.shape[0])):
        field = jnp.einsum('nkr,nvr->nvk', trans[offset:offset + width], jnp.repeat(field, 2, axis=0), precision=HIGH)
    return field + leaf_terms


def reference(vectors, self_blocks, near_blocks, near_row, near_col, bases, transfers, far_row, far_col, couplings, root_couplings):
    devices = N_SUB * N_LVL
    total = LEAF_DEV * devices
    xs = vectors.astype(jnp.float32)
    trans_dev = transfers.reshape(devices, 2 * LEAF_DEV - 2, RANK, RANK)

    def local_work(items):
        x_dev, self_dev, base_dev, trans_one = items
        self_out = jnp.einsum('lij,lvj->lvi', self_dev.astype(jnp.float32), x_dev, precision=HIGH)
        coeff = jnp.einsum('lvi,lik->lvk', x_dev, base_dev.astype(jnp.float32), precision=HIGH)
        return self_out, coeff, tree_up(coeff, trans_one)

    self_out, coeff, roots = lax.map(local_work, (xs.reshape(devices, LEAF_DEV, 2, LEAF), self_blocks.reshape(devices, LEAF_DEV, LEAF, LEAF), bases.reshape(devices, LEAF_DEV, LEAF, RANK), trans_dev))
    owner = (jnp.arange(NEAR, dtype=jnp.int32) // NEAR_DEV).astype(jnp.int32)
    row_leaf = (owner * LEAF_DEV + near_row).astype(jnp.int32)
    col_leaf = ((owner * LEAF_DEV + near_col) % total).astype(jnp.int32)

    def near_work(items):
        block, rows, cols = items
        block = block.astype(jnp.float32)
        forward = jnp.einsum('pij,pvj->pvi', block, xs[cols], precision=HIGH)
        backward = jnp.einsum('pij,pvi->pvj', block, xs[rows], precision=HIGH)
        return forward, backward

    forward, backward = lax.map(near_work, (near_blocks.reshape(devices, NEAR_DEV, LEAF, LEAF), row_leaf.reshape(devices, NEAR_DEV), col_leaf.reshape(devices, NEAR_DEV)))
    near_part = self_out.reshape(total, 2, LEAF)
    near_part = near_part.at[row_leaf].add(forward.reshape(NEAR, 2, LEAF))
    near_part = near_part.at[col_leaf].add(backward.reshape(NEAR, 2, LEAF))
    flat = coeff.reshape(total, 2, RANK)
    far_owner = (jnp.arange(FAR, dtype=jnp.int32) // FAR_DEV).astype(jnp.int32)
    far_rows = (far_owner * LEAF_DEV + far_row).astype(jnp.int32)
    far_forward = jnp.einsum('prk,pvk->pvr', couplings, flat[far_col], precision=HIGH)
    far_backward = jnp.einsum('prk,pvr->pvk', couplings, flat[far_rows], precision=HIGH)
    leaf_field = jnp.zeros((total, 2, RANK), jnp.float32).at[far_rows].add(far_forward).at[far_col].add(far_backward)
    root_field = jnp.einsum('derk,evk->dvr', root_couplings, roots, precision=HIGH)

    def down_work(items):
        top, terms, trans_one = items
        return tree_down(top, terms, trans_one)

    field = lax.map(down_work, (root_field, leaf_field.reshape(devices, LEAF_DEV, 2, RANK), trans_dev))
    field = field.reshape(total, 2, RANK).astype(jnp.bfloat16)
    far_part = jnp.einsum('lik,lvk->lvi', bases.astype(jnp.float32), field.astype(jnp.float32), precision=HIGH)
    return near_part + far_part
```

```python
import jax
import jax.numpy as jnp
from jax import lax
from jax.experimental import pallas as pl
from jax.experimental.pallas import tpu as pltpu
from jax.sharding import PartitionSpec as P

AXES = ("sub", "lvl")
F32 = jnp.float32
BF16 = jnp.bfloat16
NN = (((1,), (0,)), ((), ()))
NT = (((1,), (1,)), ((), ()))


def from_behind(x, by):
    devices = lax.axis_size(AXES)
    return lax.ppermute(x, AXES, [(i, (i + by) % devices) for i in range(devices)])


def iota(shape, dim):
    return lax.broadcasted_iota(jnp.int32, shape, dim)


def mul(a, b, dims):
    return lax.dot_general(a, b, dims, preferred_element_type=F32)


def split(x):
    high = x.astype(BF16)
    return high, (x - high.astype(F32)).astype(BF16)


def mul_split(a, b, dims):
    a_high, a_low = split(a)
    b_high, b_low = split(b)
    rows = a.shape[0]
    both = mul(jnp.concatenate([a_high, a_low], axis=0), b_high, dims)
    return both[:rows] + both[rows:] + mul(a_high, b_low, dims)


def mul_exact_left(a, b, dims):
    b_high, b_low = split(b)
    return mul(a, b_high, dims) + mul(a, b_low, dims)


def turn(x):
    rows = x.shape[0]
    if rows < 128:
        x = jnp.concatenate([x, jnp.zeros((128 - rows, x.shape[1]), x.dtype)], axis=0)
    return x.T


def swap_halves(x):
    return pltpu.roll(x, x.shape[-1] // 2, x.ndim - 1)


def chosen(condition):
    return jnp.where(condition, 1.0, 0.0).astype(BF16)


def reverse_bits(x, bits):
    out = jnp.zeros_like(x)
    for b in range(bits):
        out = out | (((x >> b) & 1) << (bits - 1 - b))
    return out


def own_leaf(rows, wide, count):
    leaf = lax.rem(iota((rows, wide), 0), count)
    half = iota((rows, wide), 1) // (wide // 2)
    return leaf, half


def start_all(pairs, sems):
    copies = [pltpu.make_async_copy(src, dst, sems.at[i]) for i, (src, dst) in enumerate(pairs)]
    for copy in copies:
        copy.start()
    return copies


def pack_kernel(
    row_in, col_in, x_in, bases_in, trans_in, coup_in, out, far_row, far_col, x, bases, trans, coup, sems
):
    devices, _, wide = out.shape
    count = x.shape[0]
    rows = 2 * count
    rank = wide // 2
    pairs = far_row.shape[1]
    cap = count // 2
    per_row = wide // cap
    copies = start_all(
        [
            (col_in, far_col),
            (row_in, far_row),
            (x_in, x),
            (bases_in, bases),
            (coup_in, coup),
            (trans_in, trans),
        ],
        sems,
    )

    me = lax.axis_index(AXES)
    copies[0].wait()
    dev = far_col[...] // count
    leaf = lax.rem(far_col[...], count)
    dev_along = jnp.broadcast_to(dev.astype(F32), (pairs, pairs))
    earlier = iota((pairs, pairs), 0) < iota((pairs, pairs), 1)
    same = (dev_along == dev_along.T) & earlier
    place = jnp.sum(same.astype(F32), axis=0, keepdims=True).astype(jnp.int32)
    seat = dev * cap + place
    at_seat = jnp.where(iota((devices * cap, pairs), 0) == seat, 1.0, 0.0).astype(BF16)
    of_dev = jnp.where(iota((devices, pairs), 0) == dev, leaf.astype(F32), 0.0).astype(BF16)
    lane_of = place + lax.rem(me, per_row) * cap
    at_lane = jnp.where(iota((wide, pairs), 0) == lane_of, 1.0, 0.0).astype(BF16)
    ids = mul(of_dev, at_lane, NT)
    copies[1].wait()
    bits = count.bit_length() - 1
    of_row = chosen(iota((wide, pairs), 0) == reverse_bits(far_row[...], bits))
    line = iota((rows, rows), 0)
    lane = iota((rows, rows), 1)
    order = reverse_bits(lax.rem(line, count), bits)
    turn_rows = chosen((line // count == lane // count) & (order == lax.rem(lane, count)))

    copies[2].wait()
    turned_x = jnp.concatenate([x[:, 0, :], x[:, 1, :]], axis=0)
    turned_x = mul(turn_rows, turned_x, NN).astype(BF16)
    copies[3].wait()
    prod = mul(turned_x, bases[...], NT)
    row_leaf, half = own_leaf(rows, wide, count)
    row_leaf = reverse_bits(row_leaf, bits)
    coeff = jnp.zeros((rows, wide), F32)
    for c in range(count // 2):
        piece = jnp.where(row_leaf == 2 * c + half, prod[:, c * wide : (c + 1) * wide], 0.0)
        coeff = coeff + piece
    coeff = coeff + swap_halves(coeff)
    half_one = iota((count, wide), 1) < rank
    flat = jnp.where(half_one, coeff[:count], coeff[count:])
    flat_b = flat.astype(BF16)
    for e in range(devices):
        first = e % 2 * cap
        out[e, :cap, :] = flat_b[first : first + cap]

    turned = jnp.concatenate([flat, jnp.zeros((wide - count, wide), F32)], axis=0).T
    t_high, t_low = split(turned)
    picked = mul(t_high, of_row, NN) + mul(t_low, of_row, NN)
    copies[4].wait()
    copies[5].wait()
    acc0 = jnp.zeros((rank, pairs), F32)
    acc1 = jnp.zeros((rank, pairs), F32)
    offset = 0
    width = count
    done = 0
    nodes = [coeff[:count], coeff[count:]]
    while width > 1:
        parents = width // 2
        span = max(8, parents)
        low = iota((span, wide), 1) < rank
        if parents >= 8:
            pairs_of = [jnp.where(low, n[:parents], n[parents:]) for n in nodes]
        else:
            pairs_of = [jnp.where(low, n, pltpu.roll(n, span - parents, 0)) for n in nodes]
        high, rest = split(jnp.concatenate(pairs_of, axis=0))
        left = jnp.concatenate([high.astype(F32), rest.astype(F32)], axis=0)
        row = lax.rem(iota(left.shape, 0), span)
        node = jnp.where(row < parents, reverse_bits(row, parents.bit_length() - 1), -1)
        left = jnp.concatenate(
            [jnp.where(node == c, left, 0.0).astype(BF16) for c in range(parents)], axis=1
        )
        mats_high, mats_low = split(trans[offset : offset + width].reshape(width * rank, rank))
        up = mul(left, mats_high, NN)
        up = up[: 2 * span] + up[2 * span :] + mul(left[: 2 * span], mats_low, NN)
        until = rank if width == 2 else done + rank // 5
        for r in range(done, until):
            block = coup[r]
            acc0 = acc0 + block * picked[r : r + 1]
            acc1 = acc1 + block * picked[rank + r : rank + r + 1]
        done = until
        up = jnp.concatenate([up, up], axis=1)
        nodes = [up[:span], up[span:]]
        offset += width
        width = parents
    terms = jnp.concatenate([acc0, acc1], axis=0).astype(BF16)
    seated = mul(at_seat, terms, NT).astype(BF16)
    for e in range(devices):
        out[e, cap : 2 * cap, :] = seated[e * cap : (e + 1) * cap]
    root = jnp.where(iota((1, wide), 1) < rank, nodes[0][0:1], nodes[1][0:1])
    root_high, root_low = split(root)
    sub = iota((8, wide), 0)
    tail = jnp.where(
        sub == 0,
        root_high.astype(F32),
        jnp.where(sub == 1, root_low.astype(F32), 0.0),
    )
    for e in range(devices):
        out[e, 2 * cap :, :] = jnp.where(sub == 2, ids[e : e + 1], tail).astype(BF16)


def column(ids):
    wide = ids.shape[1]
    if wide < 128:
        ids = jnp.concatenate([ids, jnp.zeros((1, 128 - wide), jnp.int32)], axis=1)
    return jnp.broadcast_to(ids.astype(F32), (128, 128)).T


def by_seat(col, pairs):
    parts = []
    for g in range(pairs // 8):
        parts += [col[8 * g : 8 * g + 8]] * 2
    return jnp.concatenate(parts, axis=0)


def along_seats(seat_col):
    rows = seat_col.shape[0]
    if rows < 128:
        seat_col = jnp.concatenate([seat_col, jnp.zeros((128 - rows, 128), F32)], axis=0)
    return seat_col.T.astype(jnp.int32)


def products(left, blocks, group, dims):
    member = lax.rem(iota((16, blocks.shape[2]), 0), 8)
    acc = jnp.zeros((16, blocks.shape[2]), F32)
    some = left[16 * group : 16 * group + 16]
    for j in range(8):
        acc = jnp.where(member == j, mul(some, blocks[8 * group + j], dims), acc)
    return acc


def seat_grid(shape, dim):
    seat = iota(shape, dim)
    return lax.rem(seat // 8, 2), (seat // 16) * 8 + lax.rem(seat, 8)


def near_back_kernel(
    row_in, col_in, x_in, blocks_in, own, back, near_row, near_col, x, blocks, sems
):
    pairs = blocks.shape[0]
    count = x.shape[0]
    rows = 2 * count
    seats = 2 * pairs
    parts = pairs // 8
    spans = [pl.ds(8 * g, 8) for g in range(parts)]
    copies = start_all(
        [(row_in, near_row), (col_in, near_col), (x_in, x)]
        + [(blocks_in.at[span], blocks.at[span]) for span in spans],
        sems,
    )
    for i in range(3):
        copies[i].wait()
    here = jnp.concatenate([x[:, 0, :], x[:, 1, :]], axis=0)
    row_seat = by_seat(column(near_row[...]), pairs).astype(jnp.int32)
    col_along = along_seats(by_seat(column(near_col[...]), pairs))
    lane = iota((seats, rows), 1)
    seat_v, _ = seat_grid((seats, rows), 0)
    same = (seat_v == lane // count) & (row_seat[:, :rows] == lax.rem(lane, count))
    of_row = mul(chosen(same), here, NN).astype(BF16)
    backward = []
    for g in range(parts):
        copies[3 + g].wait()
        backward.append(products(of_row, blocks, g, NN))
    backward = jnp.concatenate(backward, axis=0)

    line = iota((rows, seats), 0)
    seat_v, _ = seat_grid((rows, seats), 1)
    same_v = seat_v == line // count
    leaf = lax.rem(line, count)
    col_seat = col_along[:rows, :seats]
    to_next = chosen(same_v & (col_seat == leaf + count))
    back[...] = mul_exact_left(to_next, backward, NN).astype(BF16)
    own[...] = mul_exact_left(chosen(same_v & (col_seat == leaf)), backward, NN)


def near_main_kernel(
    row_in, col_in, x_in, after_in, own_in, blocks_in, selfs_in, own, near_row, near_col, x, after, blocks, selfs, sems
):
    pairs = blocks.shape[0]
    count = x.shape[0]
    rows = 2 * count
    seats = 2 * pairs
    parts = pairs // 8
    spans = [pl.ds(8 * g, 8) for g in range(parts)]
    copies = start_all(
        [(row_in, near_row), (col_in, near_col), (x_in, x), (after_in, after)]
        + [(selfs_in.at[span], selfs.at[span]) for span in spans]
        + [(blocks_in.at[span], blocks.at[span]) for span in spans],
        sems,
    )
    for i in range(4):
        copies[i].wait()
    both = jnp.concatenate([part[:, v, :] for part in (x, after) for v in range(2)], axis=0)
    row_along = along_seats(by_seat(column(near_row[...]), pairs))
    col_seat = by_seat(column(near_col[...]), pairs).astype(jnp.int32)
    lane = iota((seats, 2 * rows), 1)
    seat_v, seat_pair = seat_grid((seats, 2 * rows), 0)
    same_v = seat_v == lax.rem(lane // count, 2)
    leaf = (lane // rows) * count + lax.rem(lane, count)
    of_col = mul(chosen(same_v & (col_seat == leaf)), both, NN).astype(BF16)
    of_self = mul(chosen(same_v & (seat_pair == leaf)), both, NN).astype(BF16)
    forward, selfward = [], []
    for g in range(parts):
        copies[4 + g].wait()
        selfward.append(products(of_self, selfs, g, NT))
    for g in range(parts):
        copies[4 + parts + g].wait()
        forward.append(products(of_col, blocks, g, NT))

    line = iota((rows, seats), 0)
    seat_v, seat_pair = seat_grid((rows, seats), 1)
    same_v = seat_v == line // count
    leaf = lax.rem(line, count)
    spots = jnp.concatenate(
        [
            jnp.where(same_v & (row_along[:rows, :seats] == leaf), 1.0, 0.0),
            jnp.where(same_v & (seat_pair == leaf), 1.0, 0.0),
        ],
        axis=1,
    ).astype(BF16)
    own[...] = own_in[...] + mul_exact_left(spots, jnp.concatenate(forward + selfward, axis=0), NN)


def chains_kernel(trans, chains):
    count = trans.shape[0] // 2 + 1
    rank = trans.shape[1]
    low = iota((rank, 2 * rank), 1) < rank
    width = 2
    offset = trans.shape[0] - 2
    paths = [jnp.concatenate([trans[offset + n]] * 2, axis=1) for n in range(2)]
    while width < count:
        width *= 2
        offset -= width
        lower = []
        for path, first in zip(paths, range(offset, offset + width, 2)):
            left = jnp.concatenate(
                split(trans[first : first + 2].reshape(2 * rank, rank)), axis=1
            )
            high, rest = split(path)
            high = high.astype(F32)
            right = jnp.concatenate(
                [jnp.where(low, high, rest.astype(F32)), jnp.where(low, high, 0.0)], axis=0
            ).astype(BF16)
            prod = mul(left, right, NN)
            prod = prod + swap_halves(prod)
            lower += [prod[:rank], prod[rank:]]
        paths = lower
    for c in range(count // 2):
        both = []
        for path in paths[2 * c : 2 * c + 2]:
            high, rest = split(path)
            both.append(jnp.where(low, high.astype(F32), rest.astype(F32)))
        chains[:, c * 2 * rank : (c + 1) * 2 * rank] = jnp.concatenate(both, axis=0).T.astype(BF16)


def partner_rows(far_col, ref, side, count):
    pairs = far_col.shape[1]
    devices, _, wide = ref.shape
    cap = count // 2
    per = wide // cap
    col = column(far_col[...]).astype(jnp.int32)
    leaf = reverse_bits(lax.rem(col, count), count.bit_length() - 1)
    spot = jnp.where(leaf // cap == side, col // count * cap + lax.rem(leaf, cap), -1)
    rows = jnp.zeros((pairs, wide), F32)
    for g in range(devices // per):
        block = ref[g * per : (g + 1) * per, :cap, :].reshape(wide, wide)
        rows = rows + mul(chosen(iota((pairs, wide), 1) + g * wide == spot), block, NN)
    return rows


def collect_kernel(
    col_in, got_in, chains_in, root_in, own, returned, _, partner, arrived, down, near, far_col, got, chains, roots, sems
):
    devices, _, wide = got.shape
    count = arrived.shape[0]
    rank = wide // 2
    cap = count // 2
    per_row = wide // cap
    copies = start_all(
        [(got_in, got), (col_in, far_col), (root_in, roots), (chains_in, chains)], sems
    )
    near[...] = own[...] + returned[...].astype(F32)
    copies[0].wait()
    copies[1].wait()

    tail = got[:, 2 * cap :, :].astype(F32)
    sums = jnp.zeros((count, wide), F32)
    for g in range(devices // per_row):
        ids = jnp.sum(tail[g * per_row : (g + 1) * per_row, 2], axis=0, keepdims=True)
        at = chosen(iota((count, wide), 0) == ids.astype(jnp.int32))
        block = got[g * per_row : (g + 1) * per_row, cap : 2 * cap, :].reshape(wide, wide)
        sums = sums + mul(at, block, NN)
    arrived[...] = sums

    partner[...] = partner_rows(far_col, got, lax.rem(lax.axis_index(AXES), 2), count)

    root_rows = tail[:, 0] + tail[:, 1]
    second = swap_halves(root_rows)
    copies[2].wait()
    acc0 = jnp.zeros((rank, rank), F32)
    acc1 = jnp.zeros((rank, rank), F32)
    for e in range(devices):
        block = roots[e]
        acc0 = acc0 + block * root_rows[e : e + 1, :rank]
        acc1 = acc1 + block * second[e : e + 1, :rank]

    sums = jnp.concatenate([acc0, acc1], axis=1)
    of_v = chosen(iota((16, wide), 0) // 8 == iota((16, wide), 1) // rank)
    top = mul_exact_left(of_v, sums, NT)
    top = jnp.concatenate(split(top), axis=0)
    copies[3].wait()
    both = mul(jnp.concatenate([top, top], axis=1), chains[...], NN)
    down[...] = both[:16] + both[16:]


def finish_kernel(
    far_row,
    far_col,
    sibling_in,
    partner_in,
    arrived,
    down,
    near,
    bases,
    coup,
    out,
    sibling,
    ahead,
    sems,
):
    _, _, wide = sibling.shape
    rows = near.shape[0]
    count = rows // 2
    rank = wide // 2
    pairs = far_row.shape[1]
    start_all([(sibling_in.at[:, pl.ds(0, sibling.shape[1])], sibling)], sems)[0].wait()
    side = 1 - lax.rem(lax.axis_index(AXES), 2)
    partner = (partner_in[...] + partner_rows(far_col, sibling, side, count)).T

    for r in range(rank):
        block = coup[r]
        ahead[r : r + 1, :] = jnp.sum(block * partner[:rank], axis=0, keepdims=True)
        ahead[rank + r : rank + r + 1, :] = jnp.sum(block * partner[rank:], axis=0, keepdims=True)
    of_row = chosen(iota((count, pairs), 0) == far_row[...])
    leaf_field = arrived[...] + mul_exact_left(of_row, ahead[...], NT)

    leaf_rows = jnp.concatenate([leaf_field, swap_halves(leaf_field)], axis=0)
    leaf_both = jnp.where(iota((rows, wide), 1) < rank, leaf_rows, swap_halves(leaf_rows))
    row_leaf, half = own_leaf(rows, wide, count)
    first = iota((rows, wide), 0) < count
    left = []
    for c in range(count // 2):
        part = down[:, c * wide : (c + 1) * wide]
        part = jnp.where(first, part[0:1], part[8:9]) + leaf_both
        left.append(jnp.where(row_leaf == 2 * c + half, part, 0.0).astype(BF16))
    total = near[...] + mul(jnp.concatenate(left, axis=1), bases[...], NN)
    for v in range(2):
        out[:, v, :] = total[v * count : (v + 1) * count]


def vmem(x):
    return pltpu.VMEM(x.shape, x.dtype)


IN_VMEM = pl.BlockSpec(memory_space=pltpu.VMEM)
IN_HBM = pl.BlockSpec(memory_space=pltpu.HBM)
ANYWHERE = pl.BlockSpec(memory_space=pl.ANY)
ALL = pltpu.CompilerParams(vmem_limit_bytes=60 * 1024 * 1024)
MOST = pltpu.CompilerParams(vmem_limit_bytes=53 * 1024 * 1024)
SOME = pltpu.CompilerParams(vmem_limit_bytes=40 * 1024 * 1024)


def cost(flops, moved):
    return pl.CostEstimate(flops=flops, bytes_accessed=moved, transcendentals=0)


def pack(devices, far_row, far_col, vectors, bases, trans, coup):
    count = vectors.shape[0]
    wide = 2 * trans.shape[2]
    operands = (far_row, far_col, vectors, bases, trans, coup)
    return pl.pallas_call(
        pack_kernel,
        out_shape=jax.ShapeDtypeStruct((devices, count + 8, wide), BF16),
        in_specs=[IN_HBM] * 6,
        out_specs=IN_VMEM,
        scratch_shapes=[vmem(a) for a in operands] + [pltpu.SemaphoreType.DMA((6,))],
        compiler_params=ALL,
        cost_estimate=cost(10**7, 6 * 10**6),
        name="pack",
    )(*operands)


def near_back(near_row, near_col, x, blocks):
    count, _, leaf = x.shape
    operands = (near_row, near_col, x, blocks)
    return pl.pallas_call(
        near_back_kernel,
        out_shape=(
            jax.ShapeDtypeStruct((2 * count, leaf), F32),
            jax.ShapeDtypeStruct((2 * count, leaf), BF16),
        ),
        in_specs=[IN_HBM] * 4,
        out_specs=(IN_VMEM, IN_VMEM),
        scratch_shapes=[vmem(a) for a in operands]
        + [pltpu.SemaphoreType.DMA((3 + blocks.shape[0] // 8,))],
        compiler_params=MOST,
        cost_estimate=cost(10**7, 4 * 10**6),
        name="near_back",
    )(*operands)


def near_main(near_row, near_col, x, after, own, blocks, selfs):
    fetched = (near_row, near_col, x, after, blocks, selfs)
    return pl.pallas_call(
        near_main_kernel,
        out_shape=jax.ShapeDtypeStruct(own.shape, F32),
        in_specs=[IN_HBM] * 4 + [IN_VMEM] + [IN_HBM] * 2,
        out_specs=IN_VMEM,
        scratch_shapes=[vmem(a) for a in fetched]
        + [pltpu.SemaphoreType.DMA((4 + 2 * (blocks.shape[0] // 8),))],
        compiler_params=MOST,
        cost_estimate=cost(2 * 10**7, 8 * 10**6),
        name="near_main",
    )(near_row, near_col, x, after, own, blocks, selfs)


def multiply_chains(trans):
    nodes, rank, _ = trans.shape
    leaves = nodes // 2 + 1
    return pl.pallas_call(
        chains_kernel,
        out_shape=jax.ShapeDtypeStruct((2 * rank, leaves * rank), BF16),
        in_specs=[IN_VMEM],
        out_specs=IN_VMEM,
        compiler_params=SOME,
        cost_estimate=cost(10**7, 3 * 10**6),
        name="chains",
    )(trans)


def collect(far_col, got, chains, roots, own, returned, sign, count):
    wide = got.shape[2]
    fetched = (far_col, got, chains, roots)
    return pl.pallas_call(
        collect_kernel,
        out_shape=(
            jax.ShapeDtypeStruct((far_col.shape[1], wide), F32),
            jax.ShapeDtypeStruct((count, wide), F32),
            jax.ShapeDtypeStruct((16, chains.shape[1]), F32),
            jax.ShapeDtypeStruct(own.shape, F32),
        ),
        in_specs=[IN_HBM] * 4 + [IN_VMEM] * 2 + [ANYWHERE],
        out_specs=(IN_VMEM,) * 4,
        scratch_shapes=[vmem(a) for a in fetched] + [pltpu.SemaphoreType.DMA((4,))],
        compiler_params=MOST,
        cost_estimate=cost(10**7, 3 * 10**6),
        name="collect",
    )(far_col, got, chains, roots, own, returned, sign)


def finish(far_row, far_col, sibling, partner, arrived, down, near, bases, coup):
    count = near.shape[0] // 2
    devices, _, wide = sibling.shape
    halves = jax.ShapeDtypeStruct((devices, count // 2, wide), BF16)
    return pl.pallas_call(
        finish_kernel,
        out_shape=jax.ShapeDtypeStruct((count, 2, near.shape[1]), F32),
        in_specs=[IN_VMEM] * 2 + [IN_HBM] + [IN_VMEM] * 6,
        out_specs=IN_VMEM,
        scratch_shapes=[
            vmem(halves),
            pltpu.VMEM((wide, far_row.shape[1]), F32),
            pltpu.SemaphoreType.DMA((1,)),
        ],
        compiler_params=SOME,
        cost_estimate=cost(10**7, 5 * 10**6),
        name="finish",
    )(far_row, far_col, sibling, partner, arrived, down, near, bases, coup)


def shards(
    vectors,
    self_blocks,
    near_blocks,
    near_row,
    near_col,
    bases,
    transfers,
    far_row,
    far_col,
    couplings,
    root_couplings,
):
    count, _, leaf = vectors.shape
    rank = bases.shape[2]
    pairs = far_row.shape[0]
    devices = lax.axis_size(AXES)

    flat_bases = bases.transpose(0, 2, 1).reshape(count * rank, leaf)
    coup = couplings.transpose(1, 2, 0)
    far = (far_row.reshape(1, pairs), far_col.reshape(1, pairs))
    near = (near_row.reshape(1, -1), near_col.reshape(1, -1))
    following = from_behind(vectors, -1)
    payload = pack(devices, *far, vectors, flat_bases, transfers, coup)
    payload, following, x = lax.optimization_barrier((payload, following, vectors))
    got = lax.all_to_all(payload, AXES, 0, 0, tiled=True)
    own, back = near_back(*near, x, near_blocks)
    returned = from_behind(back, 1)
    own = near_main(*near, x, following, own, near_blocks, self_blocks)
    own, late_transfers = lax.optimization_barrier((own, transfers))
    chains = multiply_chains(late_transfers)
    got, chains, sign = lax.optimization_barrier((got, chains, returned[:8]))
    sibling = lax.ppermute(got, AXES, [(i, i ^ 1) for i in range(devices)])
    partner, arrived, down, near_sum = collect(
        far[1], got, chains, root_couplings[0], own, returned, sign, count
    )
    return finish(*far, sibling, partner, arrived, down, near_sum, flat_bases, coup)


def solution(mesh):
    in_specs = (
        P(AXES, None, None),
        P(AXES, None, None),
        P(AXES, None, None),
        P(AXES),
        P(AXES),
        P(AXES, None, None),
        P(AXES, None, None),
        P(AXES),
        P(AXES),
        P(AXES, None, None),
        P(AXES, None, None, None),
    )
    out_specs = P(AXES, None, None)
    return jax.shard_map(shards, mesh=mesh, in_specs=in_specs, out_specs=out_specs, check_vma=False)
```

```python
import jax
import jax.numpy as jnp
from jax import lax
from jax.experimental import pallas as pl
from jax.experimental.pallas import tpu as pltpu
from jax.sharding import PartitionSpec as P

AXES = ("sub", "lvl")
F32 = jnp.float32
BF16 = jnp.bfloat16
NN = (((1,), (0,)), ((), ()))
NT = (((1,), (1,)), ((), ()))


def from_behind(x, by):
    devices = lax.axis_size(AXES)
    return lax.ppermute(x, AXES, [(i, (i + by) % devices) for i in range(devices)])


def iota(shape, dim):
    return lax.broadcasted_iota(jnp.int32, shape, dim)


def mul(a, b, dims):
    return lax.dot_general(a, b, dims, preferred_element_type=F32)


def split(x):
    high = x.astype(BF16)
    return high, (x - high.astype(F32)).astype(BF16)


def mul_split(a, b, dims):
    a_high, a_low = split(a)
    b_high, b_low = split(b)
    rows = a.shape[0]
    both = mul(jnp.concatenate([a_high, a_low], axis=0), b_high, dims)
    return both[:rows] + both[rows:] + mul(a_high, b_low, dims)


def mul_exact_left(a, b, dims):
    b_high, b_low = split(b)
    return mul(a, b_high, dims) + mul(a, b_low, dims)


def turn(x):
    rows = x.shape[0]
    if rows < 128:
        x = jnp.concatenate([x, jnp.zeros((128 - rows, x.shape[1]), x.dtype)], axis=0)
    return x.T


def swap_halves(x):
    return pltpu.roll(x, x.shape[-1] // 2, x.ndim - 1)


def chosen(condition):
    return jnp.where(condition, 1.0, 0.0).astype(BF16)


def reverse_bits(x, bits):
    out = jnp.zeros_like(x)
    for b in range(bits):
        out = out | (((x >> b) & 1) << (bits - 1 - b))
    return out


def own_leaf(rows, wide, count):
    leaf = lax.rem(iota((rows, wide), 0), count)
    half = iota((rows, wide), 1) // (wide // 2)
    return leaf, half


def start_all(pairs, sems):
    copies = [pltpu.make_async_copy(src, dst, sems.at[i]) for i, (src, dst) in enumerate(pairs)]
    for copy in copies:
        copy.start()
    return copies


def pack_kernel(
    row_in, col_in, x_in, bases_in, trans_in, coup_in, out, far_row, far_col, x, bases, trans, coup, sems
):
    devices, _, wide = out.shape
    count = x.shape[0]
    rows = 2 * count
    rank = wide // 2
    pairs = far_row.shape[1]
    cap = count // 2
    per_row = wide // cap
    copies = start_all(
        [
            (col_in, far_col),
            (row_in, far_row),
            (x_in, x),
            (bases_in, bases),
            (coup_in, coup),
            (trans_in, trans),
        ],
        sems,
    )

    me = lax.axis_index(AXES)
    copies[0].wait()
    dev = far_col[...] // count
    leaf = lax.rem(far_col[...], count)
    dev_along = jnp.broadcast_to(dev.astype(F32), (pairs, pairs))
    earlier = iota((pairs, pairs), 0) < iota((pairs, pairs), 1)
    same = (dev_along == dev_along.T) & earlier
    place = jnp.sum(same.astype(F32), axis=0, keepdims=True).astype(jnp.int32)
    seat = dev * cap + place
    at_seat = jnp.where(iota((devices * cap, pairs), 0) == seat, 1.0, 0.0).astype(BF16)
    of_dev = jnp.where(iota((devices, pairs), 0) == dev, leaf.astype(F32), 0.0).astype(BF16)
    lane_of = place + lax.rem(me, per_row) * cap
    at_lane = jnp.where(iota((wide, pairs), 0) == lane_of, 1.0, 0.0).astype(BF16)
    ids = mul(of_dev, at_lane, NT)
    copies[1].wait()
    bits = count.bit_length() - 1
    of_row = chosen(iota((wide, pairs), 0) == reverse_bits(far_row[...], bits))
    line = iota((rows, rows), 0)
    lane = iota((rows, rows), 1)
    order = reverse_bits(lax.rem(line, count), bits)
    turn_rows = chosen((line // count == lane // count) & (order == lax.rem(lane, count)))

    copies[2].wait()
    turned_x = jnp.concatenate([x[:, 0, :], x[:, 1, :]], axis=0)
    turned_x = mul(turn_rows, turned_x, NN).astype(BF16)
    copies[3].wait()
    prod = mul(turned_x, bases[...], NT)
    row_leaf, half = own_leaf(rows, wide, count)
    row_leaf = reverse_bits(row_leaf, bits)
    coeff = jnp.zeros((rows, wide), F32)
    for c in range(count // 2):
        piece = jnp.where(row_leaf == 2 * c + half, prod[:, c * wide : (c + 1) * wide], 0.0)
        coeff = coeff + piece
    coeff = coeff + swap_halves(coeff)
    half_one = iota((count, wide), 1) < rank
    flat = jnp.where(half_one, coeff[:count], coeff[count:])
    flat_b = flat.astype(BF16)
    for e in range(devices):
        first = e % 2 * cap
        out[e, :cap, :] = flat_b[first : first + cap]

    turned = jnp.concatenate([flat, jnp.zeros((wide - count, wide), F32)], axis=0).T
    t_high, t_low = split(turned)
    picked = mul(t_high, of_row, NN) + mul(t_low, of_row, NN)
    copies[4].wait()
    copies[5].wait()
    acc0 = jnp.zeros((rank, pairs), F32)
    acc1 = jnp.zeros((rank, pairs), F32)
    offset = 0
    width = count
    done = 0
    nodes = [coeff[:count], coeff[count:]]
    while width > 1:
        parents = width // 2
        span = max(8, parents)
        low = iota((span, wide), 1) < rank
        if parents >= 8:
            pairs_of = [jnp.where(low, n[:parents], n[parents:]) for n in nodes]
        else:
            pairs_of = [jnp.where(low, n, pltpu.roll(n, span - parents, 0)) for n in nodes]
        high, rest = split(jnp.concatenate(pairs_of, axis=0))
        left = jnp.concatenate([high.astype(F32), rest.astype(F32)], axis=0)
        row = lax.rem(iota(left.shape, 0), span)
        node = jnp.where(row < parents, reverse_bits(row, parents.bit_length() - 1), -1)
        left = jnp.concatenate(
            [jnp.where(node == c, left, 0.0).astype(BF16) for c in range(parents)], axis=1
        )
        mats_high, mats_low = split(trans[offset : offset + width].reshape(width * rank, rank))
        up = mul(left, mats_high, NN)
        up = up[: 2 * span] + up[2 * span :] + mul(left[: 2 * span], mats_low, NN)
        until = rank if width == 2 else done + rank // 5
        for r in range(done, until):
            block = coup[r]
            acc0 = acc0 + block * picked[r : r + 1]
            acc1 = acc1 + block * picked[rank + r : rank + r + 1]
        done = until
        up = jnp.concatenate([up, up], axis=1)
        nodes = [up[:span], up[span:]]
        offset += width
        width = parents
    terms = jnp.concatenate([acc0, acc1], axis=0).astype(BF16)
    seated = mul(at_seat, terms, NT).astype(BF16)
    for e in range(devices):
        out[e, cap : 2 * cap, :] = seated[e * cap : (e + 1) * cap]
    root = jnp.where(iota((1, wide), 1) < rank, nodes[0][0:1], nodes[1][0:1])
    root_high, root_low = split(root)
    sub = iota((8, wide), 0)
    tail = jnp.where(
        sub == 0,
        root_high.astype(F32),
        jnp.where(sub == 1, root_low.astype(F32), 0.0),
    )
    for e in range(devices):
        out[e, 2 * cap :, :] = jnp.where(sub == 2, ids[e : e + 1], tail).astype(BF16)


def column(ids):
    wide = ids.shape[1]
    if wide < 128:
        ids = jnp.concatenate([ids, jnp.zeros((1, 128 - wide), jnp.int32)], axis=1)
    return jnp.broadcast_to(ids.astype(F32), (128, 128)).T


def by_seat(col, pairs):
    parts = []
    for g in range(pairs // 8):
        parts += [col[8 * g : 8 * g + 8]] * 2
    return jnp.concatenate(parts, axis=0)


def along_seats(seat_col):
    rows = seat_col.shape[0]
    if rows < 128:
        seat_col = jnp.concatenate([seat_col, jnp.zeros((128 - rows, 128), F32)], axis=0)
    return seat_col.T.astype(jnp.int32)


def products(left, blocks, group, dims):
    member = lax.rem(iota((16, blocks.shape[2]), 0), 8)
    acc = jnp.zeros((16, blocks.shape[2]), F32)
    some = left[16 * group : 16 * group + 16]
    for j in range(8):
        acc = jnp.where(member == j, mul(some, blocks[8 * group + j], dims), acc)
    return acc


def seat_grid(shape, dim):
    seat = iota(shape, dim)
    return lax.rem(seat // 8, 2), (seat // 16) * 8 + lax.rem(seat, 8)


def near_back_kernel(
    row_in, col_in, x_in, blocks_in, own, back, near_row, near_col, x, blocks, sems
):
    pairs = blocks.shape[0]
    count = x.shape[0]
    rows = 2 * count
    seats = 2 * pairs
    parts = pairs // 8
    spans = [pl.ds(8 * g, 8) for g in range(parts)]
    copies = start_all(
        [(row_in, near_row), (col_in, near_col), (x_in, x)]
        + [(blocks_in.at[span], blocks.at[span]) for span in spans],
        sems,
    )
    for i in range(3):
        copies[i].wait()
    here = jnp.concatenate([x[:, 0, :], x[:, 1, :]], axis=0)
    row_seat = by_seat(column(near_row[...]), pairs).astype(jnp.int32)
    col_along = along_seats(by_seat(column(near_col[...]), pairs))
    lane = iota((seats, rows), 1)
    seat_v, _ = seat_grid((seats, rows), 0)
    same = (seat_v == lane // count) & (row_seat[:, :rows] == lax.rem(lane, count))
    of_row = mul(chosen(same), here, NN).astype(BF16)
    backward = []
    for g in range(parts):
        copies[3 + g].wait()
        backward.append(products(of_row, blocks, g, NN))
    backward = jnp.concatenate(backward, axis=0)

    line = iota((rows, seats), 0)
    seat_v, _ = seat_grid((rows, seats), 1)
    same_v = seat_v == line // count
    leaf = lax.rem(line, count)
    col_seat = col_along[:rows, :seats]
    to_next = chosen(same_v & (col_seat == leaf + count))
    back[...] = mul_exact_left(to_next, backward, NN).astype(BF16)
    own[...] = mul_exact_left(chosen(same_v & (col_seat == leaf)), backward, NN)


def near_main_kernel(
    row_in, col_in, x_in, after_in, own_in, blocks_in, selfs_in, own, near_row, near_col, x, after, blocks, selfs, sems
):
    pairs = blocks.shape[0]
    count = x.shape[0]
    rows = 2 * count
    seats = 2 * pairs
    parts = pairs // 8
    spans = [pl.ds(8 * g, 8) for g in range(parts)]
    copies = start_all(
        [(row_in, near_row), (col_in, near_col), (x_in, x), (after_in, after)]
        + [(selfs_in.at[span], selfs.at[span]) for span in spans]
        + [(blocks_in.at[span], blocks.at[span]) for span in spans],
        sems,
    )
    for i in range(4):
        copies[i].wait()
    both = jnp.concatenate([part[:, v, :] for part in (x, after) for v in range(2)], axis=0)
    row_along = along_seats(by_seat(column(near_row[...]), pairs))
    col_seat = by_seat(column(near_col[...]), pairs).astype(jnp.int32)
    lane = iota((seats, 2 * rows), 1)
    seat_v, seat_pair = seat_grid((seats, 2 * rows), 0)
    same_v = seat_v == lax.rem(lane // count, 2)
    leaf = (lane // rows) * count + lax.rem(lane, count)
    of_col = mul(chosen(same_v & (col_seat == leaf)), both, NN).astype(BF16)
    of_self = mul(chosen(same_v & (seat_pair == leaf)), both, NN).astype(BF16)
    forward, selfward = [], []
    for g in range(parts):
        copies[4 + g].wait()
        selfward.append(products(of_self, selfs, g, NT))
    for g in range(parts):
        copies[4 + parts + g].wait()
        forward.append(products(of_col, blocks, g, NT))

    line = iota((rows, seats), 0)
    seat_v, seat_pair = seat_grid((rows, seats), 1)
    same_v = seat_v == line // count
    leaf = lax.rem(line, count)
    spots = jnp.concatenate(
        [
            jnp.where(same_v & (row_along[:rows, :seats] == leaf), 1.0, 0.0),
            jnp.where(same_v & (seat_pair == leaf), 1.0, 0.0),
        ],
        axis=1,
    ).astype(BF16)
    own[...] = own_in[...] + mul_exact_left(spots, jnp.concatenate(forward + selfward, axis=0), NN)


def chains_kernel(trans, chains):
    count = trans.shape[0] // 2 + 1
    rank = trans.shape[1]
    low = iota((rank, 2 * rank), 1) < rank
    width = 2
    offset = trans.shape[0] - 2
    paths = [jnp.concatenate([trans[offset + n]] * 2, axis=1) for n in range(2)]
    while width < count:
        width *= 2
        offset -= width
        lower = []
        for path, first in zip(paths, range(offset, offset + width, 2)):
            left = jnp.concatenate(
                split(trans[first : first + 2].reshape(2 * rank, rank)), axis=1
            )
            high, rest = split(path)
            high = high.astype(F32)
            right = jnp.concatenate(
                [jnp.where(low, high, rest.astype(F32)), jnp.where(low, high, 0.0)], axis=0
            ).astype(BF16)
            prod = mul(left, right, NN)
            prod = prod + swap_halves(prod)
            lower += [prod[:rank], prod[rank:]]
        paths = lower
    for c in range(count // 2):
        both = []
        for path in paths[2 * c : 2 * c + 2]:
            high, rest = split(path)
            both.append(jnp.where(low, high.astype(F32), rest.astype(F32)))
        chains[:, c * 2 * rank : (c + 1) * 2 * rank] = jnp.concatenate(both, axis=0).T.astype(BF16)


def halves_kernel(got, _, __, ___, out):
    out[...] = got[:, : out.shape[1], :]


def partner_rows(far_col, ref, side, count):
    pairs = far_col.shape[1]
    devices, _, wide = ref.shape
    cap = count // 2
    per = wide // cap
    col = column(far_col[...]).astype(jnp.int32)
    leaf = reverse_bits(lax.rem(col, count), count.bit_length() - 1)
    spot = jnp.where(leaf // cap == side, col // count * cap + lax.rem(leaf, cap), -1)
    rows = jnp.zeros((pairs, wide), F32)
    for g in range(devices // per):
        block = ref[g * per : (g + 1) * per, :cap, :].reshape(wide, wide)
        rows = rows + mul(chosen(iota((pairs, wide), 1) + g * wide == spot), block, NN)
    return rows


def collect_kernel(
    col_in, got_in, chains_in, root_in, own, returned, partner, arrived, down, near, far_col, got, chains, roots, sems
):
    devices, _, wide = got.shape
    count = arrived.shape[0]
    rank = wide // 2
    cap = count // 2
    per_row = wide // cap
    copies = start_all(
        [(got_in, got), (col_in, far_col), (root_in, roots), (chains_in, chains)], sems
    )
    near[...] = own[...] + returned[...].astype(F32)
    copies[0].wait()
    copies[1].wait()

    tail = got[:, 2 * cap :, :].astype(F32)
    sums = jnp.zeros((count, wide), F32)
    for g in range(devices // per_row):
        ids = jnp.sum(tail[g * per_row : (g + 1) * per_row, 2], axis=0, keepdims=True)
        at = chosen(iota((count, wide), 0) == ids.astype(jnp.int32))
        block = got[g * per_row : (g + 1) * per_row, cap : 2 * cap, :].reshape(wide, wide)
        sums = sums + mul(at, block, NN)
    arrived[...] = sums

    partner[...] = partner_rows(far_col, got, lax.rem(lax.axis_index(AXES), 2), count)

    root_rows = tail[:, 0] + tail[:, 1]
    second = swap_halves(root_rows)
    copies[2].wait()
    acc0 = jnp.zeros((rank, rank), F32)
    acc1 = jnp.zeros((rank, rank), F32)
    for e in range(devices):
        block = roots[e]
        acc0 = acc0 + block * root_rows[e : e + 1, :rank]
        acc1 = acc1 + block * second[e : e + 1, :rank]

    sums = jnp.concatenate([acc0, acc1], axis=1)
    of_v = chosen(iota((16, wide), 0) // 8 == iota((16, wide), 1) // rank)
    top = mul_exact_left(of_v, sums, NT)
    top = jnp.concatenate(split(top), axis=0)
    copies[3].wait()
    both = mul(jnp.concatenate([top, top], axis=1), chains[...], NN)
    down[...] = both[:16] + both[16:]


def finish_kernel(
    far_row,
    far_col,
    sibling,
    partner_in,
    arrived,
    down,
    near,
    bases,
    coup_in,
    out,
    coup,
    ahead,
    sems,
):
    _, _, wide = sibling.shape
    rows = near.shape[0]
    count = rows // 2
    rank = wide // 2
    pairs = far_row.shape[1]
    spans = [pl.ds(16 * g, 16) for g in range(rank // 16)]
    copies = start_all([(coup_in.at[span], coup.at[span]) for span in spans], sems)
    side = 1 - lax.rem(lax.axis_index(AXES), 2)
    partner = (partner_in[...] + partner_rows(far_col, sibling, side, count)).T

    for r in range(rank):
        if r % 16 == 0:
            copies[r // 16].wait()
        block = coup[r]
        ahead[r : r + 1, :] = jnp.sum(block * partner[:rank], axis=0, keepdims=True)
        ahead[rank + r : rank + r + 1, :] = jnp.sum(block * partner[rank:], axis=0, keepdims=True)
    of_row = chosen(iota((count, pairs), 0) == far_row[...])
    leaf_field = arrived[...] + mul_exact_left(of_row, ahead[...], NT)

    leaf_rows = jnp.concatenate([leaf_field, swap_halves(leaf_field)], axis=0)
    leaf_both = jnp.where(iota((rows, wide), 1) < rank, leaf_rows, swap_halves(leaf_rows))
    row_leaf, half = own_leaf(rows, wide, count)
    first = iota((rows, wide), 0) < count
    left = []
    for c in range(count // 2):
        part = down[:, c * wide : (c + 1) * wide]
        part = jnp.where(first, part[0:1], part[8:9]) + leaf_both
        left.append(jnp.where(row_leaf == 2 * c + half, part, 0.0).astype(BF16))
    total = near[...] + mul(jnp.concatenate(left, axis=1), bases[...], NN)
    for v in range(2):
        out[:, v, :] = total[v * count : (v + 1) * count]


def vmem(x):
    return pltpu.VMEM(x.shape, x.dtype)


IN_VMEM = pl.BlockSpec(memory_space=pltpu.VMEM)
IN_HBM = pl.BlockSpec(memory_space=pltpu.HBM)
ANYWHERE = pl.BlockSpec(memory_space=pl.ANY)
ALL = pltpu.CompilerParams(vmem_limit_bytes=60 * 1024 * 1024)
MOST = pltpu.CompilerParams(vmem_limit_bytes=53 * 1024 * 1024)
SOME = pltpu.CompilerParams(vmem_limit_bytes=40 * 1024 * 1024)


def cost(flops, moved):
    return pl.CostEstimate(flops=flops, bytes_accessed=moved, transcendentals=0)


def pack(devices, far_row, far_col, vectors, bases, trans, coup):
    count = vectors.shape[0]
    wide = 2 * trans.shape[2]
    operands = (far_row, far_col, vectors, bases, trans, coup)
    return pl.pallas_call(
        pack_kernel,
        out_shape=jax.ShapeDtypeStruct((devices, count + 8, wide), BF16),
        in_specs=[IN_HBM] * 6,
        out_specs=IN_VMEM,
        scratch_shapes=[vmem(a) for a in operands] + [pltpu.SemaphoreType.DMA((6,))],
        compiler_params=ALL,
        cost_estimate=cost(10**7, 6 * 10**6),
        name="pack",
    )(*operands)


def near_back(near_row, near_col, x, blocks):
    count, _, leaf = x.shape
    operands = (near_row, near_col, x, blocks)
    return pl.pallas_call(
        near_back_kernel,
        out_shape=(
            jax.ShapeDtypeStruct((2 * count, leaf), F32),
            jax.ShapeDtypeStruct((2 * count, leaf), BF16),
        ),
        in_specs=[IN_HBM] * 4,
        out_specs=(IN_VMEM, IN_VMEM),
        scratch_shapes=[vmem(a) for a in operands]
        + [pltpu.SemaphoreType.DMA((3 + blocks.shape[0] // 8,))],
        compiler_params=MOST,
        cost_estimate=cost(10**7, 4 * 10**6),
        name="near_back",
    )(*operands)


def near_main(near_row, near_col, x, after, own, blocks, selfs):
    fetched = (near_row, near_col, x, after, blocks, selfs)
    return pl.pallas_call(
        near_main_kernel,
        out_shape=jax.ShapeDtypeStruct(own.shape, F32),
        in_specs=[IN_HBM] * 4 + [IN_VMEM] + [IN_HBM] * 2,
        out_specs=IN_VMEM,
        scratch_shapes=[vmem(a) for a in fetched]
        + [pltpu.SemaphoreType.DMA((4 + 2 * (blocks.shape[0] // 8),))],
        compiler_params=MOST,
        cost_estimate=cost(2 * 10**7, 8 * 10**6),
        name="near_main",
    )(near_row, near_col, x, after, own, blocks, selfs)


def multiply_chains(trans):
    nodes, rank, _ = trans.shape
    leaves = nodes // 2 + 1
    return pl.pallas_call(
        chains_kernel,
        out_shape=jax.ShapeDtypeStruct((2 * rank, leaves * rank), BF16),
        in_specs=[IN_VMEM],
        out_specs=IN_VMEM,
        compiler_params=SOME,
        cost_estimate=cost(10**7, 3 * 10**6),
        name="chains",
    )(trans)


def halves(got, chains, own, returned, count):
    devices, _, wide = got.shape
    return pl.pallas_call(
        halves_kernel,
        out_shape=jax.ShapeDtypeStruct((devices, count // 2, wide), BF16),
        in_specs=[IN_VMEM] + [ANYWHERE] * 3,
        out_specs=IN_VMEM,
        compiler_params=SOME,
        cost_estimate=cost(10**5, 10**5),
        name="halves",
    )(got, chains, own, returned)


def collect(far_col, got, chains, roots, own, returned, count):
    wide = got.shape[2]
    fetched = (far_col, got, chains, roots)
    return pl.pallas_call(
        collect_kernel,
        out_shape=(
            jax.ShapeDtypeStruct((far_col.shape[1], wide), F32),
            jax.ShapeDtypeStruct((count, wide), F32),
            jax.ShapeDtypeStruct((16, chains.shape[1]), F32),
            jax.ShapeDtypeStruct(own.shape, F32),
        ),
        in_specs=[IN_HBM] * 4 + [IN_VMEM] * 2,
        out_specs=(IN_VMEM,) * 4,
        scratch_shapes=[vmem(a) for a in fetched] + [pltpu.SemaphoreType.DMA((4,))],
        compiler_params=MOST,
        cost_estimate=cost(10**7, 3 * 10**6),
        name="collect",
    )(far_col, got, chains, roots, own, returned)


def finish(far_row, far_col, sibling, partner, arrived, down, near, bases, coup):
    count = near.shape[0] // 2
    wide = sibling.shape[2]
    return pl.pallas_call(
        finish_kernel,
        out_shape=jax.ShapeDtypeStruct((count, 2, near.shape[1]), F32),
        in_specs=[IN_VMEM] * 8 + [IN_HBM],
        out_specs=IN_VMEM,
        scratch_shapes=[
            vmem(coup),
            pltpu.VMEM((wide, far_row.shape[1]), F32),
            pltpu.SemaphoreType.DMA((coup.shape[0] // 16,)),
        ],
        compiler_params=pltpu.CompilerParams(vmem_limit_bytes=47 * 1024 * 1024),
        cost_estimate=cost(10**7, 5 * 10**6),
        name="finish",
    )(far_row, far_col, sibling, partner, arrived, down, near, bases, coup)


def shards(
    vectors,
    self_blocks,
    near_blocks,
    near_row,
    near_col,
    bases,
    transfers,
    far_row,
    far_col,
    couplings,
    root_couplings,
):
    count, _, leaf = vectors.shape
    rank = bases.shape[2]
    pairs = far_row.shape[0]
    devices = lax.axis_size(AXES)

    flat_bases = bases.transpose(0, 2, 1).reshape(count * rank, leaf)
    coup = couplings.transpose(1, 2, 0)
    far = (far_row.reshape(1, pairs), far_col.reshape(1, pairs))
    near = (near_row.reshape(1, -1), near_col.reshape(1, -1))
    following = from_behind(vectors, -1)
    payload = pack(devices, *far, vectors, flat_bases, transfers, coup)
    payload, following, x = lax.optimization_barrier((payload, following, vectors))
    got = lax.all_to_all(payload, AXES, 0, 0, tiled=True)
    own, back = near_back(*near, x, near_blocks)
    returned = from_behind(back, 1)
    own = near_main(*near, x, following, own, near_blocks, self_blocks)
    own, late_transfers = lax.optimization_barrier((own, transfers))
    chains = multiply_chains(late_transfers)
    mine = halves(got, chains, own, returned, count)
    sibling = lax.ppermute(mine, AXES, [(i, i ^ 1) for i in range(devices)])
    partner, arrived, down, near_sum = collect(
        far[1], got, chains, root_couplings[0], own, returned, count
    )
    return finish(*far, sibling, partner, arrived, down, near_sum, flat_bases, coup)


def solution(mesh):
    in_specs = (
        P(AXES, None, None),
        P(AXES, None, None),
        P(AXES, None, None),
        P(AXES),
        P(AXES),
        P(AXES, None, None),
        P(AXES, None, None),
        P(AXES),
        P(AXES),
        P(AXES, None, None),
        P(AXES, None, None, None),
    )
    out_specs = P(AXES, None, None)
    return jax.shard_map(shards, mesh=mesh, in_specs=in_specs, out_specs=out_specs, check_vma=False)
```

```python
import jax
import jax.numpy as jnp
from jax import lax
from jax.experimental import pallas as pl
from jax.experimental.pallas import tpu as pltpu
from jax.sharding import PartitionSpec as P

AXES = ("sub", "lvl")
F32 = jnp.float32
BF16 = jnp.bfloat16
NN = (((1,), (0,)), ((), ()))
NT = (((1,), (1,)), ((), ()))


def from_behind(x, by):
    devices = lax.axis_size(AXES)
    return lax.ppermute(x, AXES, [(i, (i + by) % devices) for i in range(devices)])


def iota(shape, dim):
    return lax.broadcasted_iota(jnp.int32, shape, dim)


def mul(a, b, dims):
    return lax.dot_general(a, b, dims, preferred_element_type=F32)


def split(x):
    high = x.astype(BF16)
    return high, (x - high.astype(F32)).astype(BF16)


def mul_split(a, b, dims):
    a_high, a_low = split(a)
    b_high, b_low = split(b)
    rows = a.shape[0]
    both = mul(jnp.concatenate([a_high, a_low], axis=0), b_high, dims)
    return both[:rows] + both[rows:] + mul(a_high, b_low, dims)


def mul_exact_left(a, b, dims):
    b_high, b_low = split(b)
    return mul(a, b_high, dims) + mul(a, b_low, dims)


def turn(x):
    rows = x.shape[0]
    if rows < 128:
        x = jnp.concatenate([x, jnp.zeros((128 - rows, x.shape[1]), x.dtype)], axis=0)
    return x.T


def swap_halves(x):
    return pltpu.roll(x, x.shape[-1] // 2, x.ndim - 1)


def chosen(condition):
    return jnp.where(condition, 1.0, 0.0).astype(BF16)


def reverse_bits(x, bits):
    out = jnp.zeros_like(x)
    for b in range(bits):
        out = out | (((x >> b) & 1) << (bits - 1 - b))
    return out


def own_leaf(rows, wide, count):
    leaf = lax.rem(iota((rows, wide), 0), count)
    half = iota((rows, wide), 1) // (wide // 2)
    return leaf, half


def start_all(pairs, sems):
    copies = [pltpu.make_async_copy(src, dst, sems.at[i]) for i, (src, dst) in enumerate(pairs)]
    for copy in copies:
        copy.start()
    return copies


def pack_kernel(
    row_in, col_in, x_in, bases_in, trans_in, coup_in, out, far_row, far_col, x, bases, trans, coup, sems
):
    devices, _, wide = out.shape
    count = x.shape[0]
    rows = 2 * count
    rank = wide // 2
    pairs = far_row.shape[1]
    cap = count // 2
    per_row = wide // cap
    copies = start_all(
        [
            (col_in, far_col),
            (row_in, far_row),
            (x_in, x),
            (bases_in, bases),
            (coup_in, coup),
            (trans_in, trans),
        ],
        sems,
    )

    me = lax.axis_index(AXES)
    copies[0].wait()
    dev = far_col[...] // count
    leaf = lax.rem(far_col[...], count)
    dev_along = jnp.broadcast_to(dev.astype(F32), (pairs, pairs))
    earlier = iota((pairs, pairs), 0) < iota((pairs, pairs), 1)
    same = (dev_along == dev_along.T) & earlier
    place = jnp.sum(same.astype(F32), axis=0, keepdims=True).astype(jnp.int32)
    seat = dev * cap + place
    at_seat = jnp.where(iota((devices * cap, pairs), 0) == seat, 1.0, 0.0).astype(BF16)
    of_dev = jnp.where(iota((devices, pairs), 0) == dev, leaf.astype(F32), 0.0).astype(BF16)
    lane_of = place + lax.rem(me, per_row) * cap
    at_lane = jnp.where(iota((wide, pairs), 0) == lane_of, 1.0, 0.0).astype(BF16)
    ids = mul(of_dev, at_lane, NT)
    copies[1].wait()
    bits = count.bit_length() - 1
    of_row = chosen(iota((wide, pairs), 0) == reverse_bits(far_row[...], bits))
    line = iota((rows, rows), 0)
    lane = iota((rows, rows), 1)
    order = reverse_bits(lax.rem(line, count), bits)
    turn_rows = chosen((line // count == lane // count) & (order == lax.rem(lane, count)))

    copies[2].wait()
    turned_x = jnp.concatenate([x[:, 0, :], x[:, 1, :]], axis=0)
    turned_x = mul(turn_rows, turned_x, NN).astype(BF16)
    copies[3].wait()
    prod = mul(turned_x, bases[...], NT)
    row_leaf, half = own_leaf(rows, wide, count)
    row_leaf = reverse_bits(row_leaf, bits)
    coeff = jnp.zeros((rows, wide), F32)
    for c in range(count // 2):
        piece = jnp.where(row_leaf == 2 * c + half, prod[:, c * wide : (c + 1) * wide], 0.0)
        coeff = coeff + piece
    coeff = coeff + swap_halves(coeff)
    half_one = iota((count, wide), 1) < rank
    flat = jnp.where(half_one, coeff[:count], coeff[count:])
    flat_b = flat.astype(BF16)
    for e in range(devices):
        first = e % 2 * cap
        out[e, :cap, :] = flat_b[first : first + cap]

    turned = jnp.concatenate([flat, jnp.zeros((wide - count, wide), F32)], axis=0).T
    t_high, t_low = split(turned)
    picked = mul(t_high, of_row, NN) + mul(t_low, of_row, NN)
    copies[4].wait()
    copies[5].wait()
    acc0 = jnp.zeros((rank, pairs), F32)
    acc1 = jnp.zeros((rank, pairs), F32)
    offset = 0
    width = count
    done = 0
    nodes = [coeff[:count], coeff[count:]]
    while width > 1:
        parents = width // 2
        span = max(8, parents)
        low = iota((span, wide), 1) < rank
        if parents >= 8:
            pairs_of = [jnp.where(low, n[:parents], n[parents:]) for n in nodes]
        else:
            pairs_of = [jnp.where(low, n, pltpu.roll(n, span - parents, 0)) for n in nodes]
        high, rest = split(jnp.concatenate(pairs_of, axis=0))
        left = jnp.concatenate([high.astype(F32), rest.astype(F32)], axis=0)
        row = lax.rem(iota(left.shape, 0), span)
        node = jnp.where(row < parents, reverse_bits(row, parents.bit_length() - 1), -1)
        left = jnp.concatenate(
            [jnp.where(node == c, left, 0.0).astype(BF16) for c in range(parents)], axis=1
        )
        mats_high, mats_low = split(trans[offset : offset + width].reshape(width * rank, rank))
        up = mul(left, mats_high, NN)
        up = up[: 2 * span] + up[2 * span :] + mul(left[: 2 * span], mats_low, NN)
        until = rank if width == 2 else done + rank // 5
        for r in range(done, until):
            block = coup[r]
            acc0 = acc0 + block * picked[r : r + 1]
            acc1 = acc1 + block * picked[rank + r : rank + r + 1]
        done = until
        up = jnp.concatenate([up, up], axis=1)
        nodes = [up[:span], up[span:]]
        offset += width
        width = parents
    terms = jnp.concatenate([acc0, acc1], axis=0).astype(BF16)
    seated = mul(at_seat, terms, NT).astype(BF16)
    for e in range(devices):
        out[e, cap : 2 * cap, :] = seated[e * cap : (e + 1) * cap]
    root = jnp.where(iota((1, wide), 1) < rank, nodes[0][0:1], nodes[1][0:1])
    root_high, root_low = split(root)
    sub = iota((8, wide), 0)
    tail = jnp.where(
        sub == 0,
        root_high.astype(F32),
        jnp.where(sub == 1, root_low.astype(F32), 0.0),
    )
    for e in range(devices):
        out[e, 2 * cap :, :] = jnp.where(sub == 2, ids[e : e + 1], tail).astype(BF16)


def column(ids):
    wide = ids.shape[1]
    if wide < 128:
        ids = jnp.concatenate([ids, jnp.zeros((1, 128 - wide), jnp.int32)], axis=1)
    return jnp.broadcast_to(ids.astype(F32), (128, 128)).T


def by_seat(col, pairs):
    parts = []
    for g in range(pairs // 8):
        parts += [col[8 * g : 8 * g + 8]] * 2
    return jnp.concatenate(parts, axis=0)


def along_seats(seat_col):
    rows = seat_col.shape[0]
    if rows < 128:
        seat_col = jnp.concatenate([seat_col, jnp.zeros((128 - rows, 128), F32)], axis=0)
    return seat_col.T.astype(jnp.int32)


def products(left, blocks, group, dims):
    member = lax.rem(iota((16, blocks.shape[2]), 0), 8)
    acc = jnp.zeros((16, blocks.shape[2]), F32)
    some = left[16 * group : 16 * group + 16]
    for j in range(8):
        acc = jnp.where(member == j, mul(some, blocks[8 * group + j], dims), acc)
    return acc


def seat_grid(shape, dim):
    seat = iota(shape, dim)
    return lax.rem(seat // 8, 2), (seat // 16) * 8 + lax.rem(seat, 8)


def near_back_kernel(
    row_in, col_in, x_in, blocks_in, own, back, near_row, near_col, x, blocks, sems
):
    pairs = blocks.shape[0]
    count = x.shape[0]
    rows = 2 * count
    seats = 2 * pairs
    parts = pairs // 8
    spans = [pl.ds(8 * g, 8) for g in range(parts)]
    copies = start_all(
        [(row_in, near_row), (col_in, near_col), (x_in, x)]
        + [(blocks_in.at[span], blocks.at[span]) for span in spans],
        sems,
    )
    for i in range(3):
        copies[i].wait()
    here = jnp.concatenate([x[:, 0, :], x[:, 1, :]], axis=0)
    row_seat = by_seat(column(near_row[...]), pairs).astype(jnp.int32)
    col_along = along_seats(by_seat(column(near_col[...]), pairs))
    lane = iota((seats, rows), 1)
    seat_v, _ = seat_grid((seats, rows), 0)
    same = (seat_v == lane // count) & (row_seat[:, :rows] == lax.rem(lane, count))
    of_row = mul(chosen(same), here, NN).astype(BF16)
    backward = []
    for g in range(parts):
        copies[3 + g].wait()
        backward.append(products(of_row, blocks, g, NN))
    backward = jnp.concatenate(backward, axis=0)

    line = iota((rows, seats), 0)
    seat_v, _ = seat_grid((rows, seats), 1)
    same_v = seat_v == line // count
    leaf = lax.rem(line, count)
    col_seat = col_along[:rows, :seats]
    to_next = chosen(same_v & (col_seat == leaf + count))
    back[...] = mul_exact_left(to_next, backward, NN).astype(BF16)
    own[...] = mul_exact_left(chosen(same_v & (col_seat == leaf)), backward, NN)


def near_main_kernel(
    row_in, col_in, x_in, after_in, own_in, blocks_in, selfs_in, own, near_row, near_col, x, after, blocks, selfs, sems
):
    pairs = blocks.shape[0]
    count = x.shape[0]
    rows = 2 * count
    seats = 2 * pairs
    parts = pairs // 8
    spans = [pl.ds(8 * g, 8) for g in range(parts)]
    copies = start_all(
        [(row_in, near_row), (col_in, near_col), (x_in, x), (after_in, after)]
        + [(selfs_in.at[span], selfs.at[span]) for span in spans]
        + [(blocks_in.at[span], blocks.at[span]) for span in spans],
        sems,
    )
    for i in range(4):
        copies[i].wait()
    both = jnp.concatenate([part[:, v, :] for part in (x, after) for v in range(2)], axis=0)
    row_along = along_seats(by_seat(column(near_row[...]), pairs))
    col_seat = by_seat(column(near_col[...]), pairs).astype(jnp.int32)
    lane = iota((seats, 2 * rows), 1)
    seat_v, seat_pair = seat_grid((seats, 2 * rows), 0)
    same_v = seat_v == lax.rem(lane // count, 2)
    leaf = (lane // rows) * count + lax.rem(lane, count)
    of_col = mul(chosen(same_v & (col_seat == leaf)), both, NN).astype(BF16)
    of_self = mul(chosen(same_v & (seat_pair == leaf)), both, NN).astype(BF16)
    forward, selfward = [], []
    for g in range(parts):
        copies[4 + g].wait()
        selfward.append(products(of_self, selfs, g, NT))
    for g in range(parts):
        copies[4 + parts + g].wait()
        forward.append(products(of_col, blocks, g, NT))

    line = iota((rows, seats), 0)
    seat_v, seat_pair = seat_grid((rows, seats), 1)
    same_v = seat_v == line // count
    leaf = lax.rem(line, count)
    spots = jnp.concatenate(
        [
            jnp.where(same_v & (row_along[:rows, :seats] == leaf), 1.0, 0.0),
            jnp.where(same_v & (seat_pair == leaf), 1.0, 0.0),
        ],
        axis=1,
    ).astype(BF16)
    own[...] = own_in[...] + mul_exact_left(spots, jnp.concatenate(forward + selfward, axis=0), NN)


def chains_kernel(trans, chains):
    count = trans.shape[0] // 2 + 1
    rank = trans.shape[1]
    low = iota((rank, 2 * rank), 1) < rank
    width = 2
    offset = trans.shape[0] - 2
    paths = [jnp.concatenate([trans[offset + n]] * 2, axis=1) for n in range(2)]
    while width < count:
        width *= 2
        offset -= width
        lower = []
        for path, first in zip(paths, range(offset, offset + width, 2)):
            left = jnp.concatenate(
                split(trans[first : first + 2].reshape(2 * rank, rank)), axis=1
            )
            high, rest = split(path)
            high = high.astype(F32)
            right = jnp.concatenate(
                [jnp.where(low, high, rest.astype(F32)), jnp.where(low, high, 0.0)], axis=0
            ).astype(BF16)
            prod = mul(left, right, NN)
            prod = prod + swap_halves(prod)
            lower += [prod[:rank], prod[rank:]]
        paths = lower
    for c in range(count // 2):
        both = []
        for path in paths[2 * c : 2 * c + 2]:
            high, rest = split(path)
            both.append(jnp.where(low, high.astype(F32), rest.astype(F32)))
        chains[:, c * 2 * rank : (c + 1) * 2 * rank] = jnp.concatenate(both, axis=0).T.astype(BF16)


def halves_kernel(got, _, __, ___, out):
    out[...] = got[:, : out.shape[1], :]


def partner_rows(far_col, ref, side, count):
    pairs = far_col.shape[1]
    devices, _, wide = ref.shape
    cap = count // 2
    per = wide // cap
    col = column(far_col[...]).astype(jnp.int32)
    leaf = reverse_bits(lax.rem(col, count), count.bit_length() - 1)
    spot = jnp.where(leaf // cap == side, col // count * cap + lax.rem(leaf, cap), -1)
    rows = jnp.zeros((pairs, wide), F32)
    for g in range(devices // per):
        block = ref[g * per : (g + 1) * per, :cap, :].reshape(wide, wide)
        rows = rows + mul(chosen(iota((pairs, wide), 1) + g * wide == spot), block, NN)
    return rows


def collect_kernel(
    col_in, got_in, chains_in, root_in, own, returned, partner, arrived, down, near, far_col, got, chains, roots, sems
):
    devices, _, wide = got.shape
    count = arrived.shape[0]
    rank = wide // 2
    cap = count // 2
    per_row = wide // cap
    copies = start_all(
        [(got_in, got), (col_in, far_col), (root_in, roots), (chains_in, chains)], sems
    )
    near[...] = own[...] + returned[...].astype(F32)
    copies[0].wait()
    copies[1].wait()

    tail = got[:, 2 * cap :, :].astype(F32)
    sums = jnp.zeros((count, wide), F32)
    for g in range(devices // per_row):
        ids = jnp.sum(tail[g * per_row : (g + 1) * per_row, 2], axis=0, keepdims=True)
        at = chosen(iota((count, wide), 0) == ids.astype(jnp.int32))
        block = got[g * per_row : (g + 1) * per_row, cap : 2 * cap, :].reshape(wide, wide)
        sums = sums + mul(at, block, NN)
    arrived[...] = sums

    partner[...] = partner_rows(far_col, got, lax.rem(lax.axis_index(AXES), 2), count)

    root_rows = tail[:, 0] + tail[:, 1]
    second = swap_halves(root_rows)
    copies[2].wait()
    acc0 = jnp.zeros((rank, rank), F32)
    acc1 = jnp.zeros((rank, rank), F32)
    for e in range(devices):
        block = roots[e]
        acc0 = acc0 + block * root_rows[e : e + 1, :rank]
        acc1 = acc1 + block * second[e : e + 1, :rank]

    sums = jnp.concatenate([acc0, acc1], axis=1)
    of_v = chosen(iota((16, wide), 0) // 8 == iota((16, wide), 1) // rank)
    top = mul_exact_left(of_v, sums, NT)
    top = jnp.concatenate(split(top), axis=0)
    copies[3].wait()
    both = mul(jnp.concatenate([top, top], axis=1), chains[...], NN)
    down[...] = both[:16] + both[16:]


def finish_kernel(
    far_row,
    far_col,
    sibling,
    partner_in,
    arrived,
    down,
    near,
    bases,
    coup_in,
    out,
    coup,
    ahead,
    sems,
):
    _, _, wide = sibling.shape
    rows = near.shape[0]
    count = rows // 2
    rank = wide // 2
    pairs = far_row.shape[1]
    spans = [pl.ds(8 * g, 8) for g in range(rank // 8)]
    copies = start_all([(coup_in.at[span], coup.at[span]) for span in spans], sems)
    side = 1 - lax.rem(lax.axis_index(AXES), 2)
    partner = (partner_in[...] + partner_rows(far_col, sibling, side, count)).T

    for r in range(rank):
        if r % 8 == 0:
            copies[r // 8].wait()
        block = coup[r]
        ahead[r : r + 1, :] = jnp.sum(block * partner[:rank], axis=0, keepdims=True)
        ahead[rank + r : rank + r + 1, :] = jnp.sum(block * partner[rank:], axis=0, keepdims=True)
    of_row = chosen(iota((count, pairs), 0) == far_row[...])
    leaf_field = arrived[...] + mul_exact_left(of_row, ahead[...], NT)

    leaf_rows = jnp.concatenate([leaf_field, swap_halves(leaf_field)], axis=0)
    leaf_both = jnp.where(iota((rows, wide), 1) < rank, leaf_rows, swap_halves(leaf_rows))
    row_leaf, half = own_leaf(rows, wide, count)
    first = iota((rows, wide), 0) < count
    left = []
    for c in range(count // 2):
        part = down[:, c * wide : (c + 1) * wide]
        part = jnp.where(first, part[0:1], part[8:9]) + leaf_both
        left.append(jnp.where(row_leaf == 2 * c + half, part, 0.0).astype(BF16))
    total = near[...] + mul(jnp.concatenate(left, axis=1), bases[...], NN)
    for v in range(2):
        out[:, v, :] = total[v * count : (v + 1) * count]


def vmem(x):
    return pltpu.VMEM(x.shape, x.dtype)


IN_VMEM = pl.BlockSpec(memory_space=pltpu.VMEM)
IN_HBM = pl.BlockSpec(memory_space=pltpu.HBM)
ANYWHERE = pl.BlockSpec(memory_space=pl.ANY)
ALL = pltpu.CompilerParams(vmem_limit_bytes=60 * 1024 * 1024)
MOST = pltpu.CompilerParams(vmem_limit_bytes=53 * 1024 * 1024)
SOME = pltpu.CompilerParams(vmem_limit_bytes=40 * 1024 * 1024)


def cost(flops, moved):
    return pl.CostEstimate(flops=flops, bytes_accessed=moved, transcendentals=0)


def pack(devices, far_row, far_col, vectors, bases, trans, coup):
    count = vectors.shape[0]
    wide = 2 * trans.shape[2]
    operands = (far_row, far_col, vectors, bases, trans, coup)
    return pl.pallas_call(
        pack_kernel,
        out_shape=jax.ShapeDtypeStruct((devices, count + 8, wide), BF16),
        in_specs=[IN_HBM] * 6,
        out_specs=IN_VMEM,
        scratch_shapes=[vmem(a) for a in operands] + [pltpu.SemaphoreType.DMA((6,))],
        compiler_params=ALL,
        cost_estimate=cost(10**7, 6 * 10**6),
        name="pack",
    )(*operands)


def near_back(near_row, near_col, x, blocks):
    count, _, leaf = x.shape
    operands = (near_row, near_col, x, blocks)
    return pl.pallas_call(
        near_back_kernel,
        out_shape=(
            jax.ShapeDtypeStruct((2 * count, leaf), F32),
            jax.ShapeDtypeStruct((2 * count, leaf), BF16),
        ),
        in_specs=[IN_HBM] * 4,
        out_specs=(IN_VMEM, IN_VMEM),
        scratch_shapes=[vmem(a) for a in operands]
        + [pltpu.SemaphoreType.DMA((3 + blocks.shape[0] // 8,))],
        compiler_params=MOST,
        cost_estimate=cost(10**7, 4 * 10**6),
        name="near_back",
    )(*operands)


def near_main(near_row, near_col, x, after, own, blocks, selfs):
    fetched = (near_row, near_col, x, after, blocks, selfs)
    return pl.pallas_call(
        near_main_kernel,
        out_shape=jax.ShapeDtypeStruct(own.shape, F32),
        in_specs=[IN_HBM] * 4 + [IN_VMEM] + [IN_HBM] * 2,
        out_specs=IN_VMEM,
        scratch_shapes=[vmem(a) for a in fetched]
        + [pltpu.SemaphoreType.DMA((4 + 2 * (blocks.shape[0] // 8),))],
        compiler_params=MOST,
        cost_estimate=cost(2 * 10**7, 8 * 10**6),
        name="near_main",
    )(near_row, near_col, x, after, own, blocks, selfs)


def multiply_chains(trans):
    nodes, rank, _ = trans.shape
    leaves = nodes // 2 + 1
    return pl.pallas_call(
        chains_kernel,
        out_shape=jax.ShapeDtypeStruct((2 * rank, leaves * rank), BF16),
        in_specs=[IN_VMEM],
        out_specs=IN_VMEM,
        compiler_params=SOME,
        cost_estimate=cost(10**7, 3 * 10**6),
        name="chains",
    )(trans)


def halves(got, chains, own, returned, count):
    devices, _, wide = got.shape
    return pl.pallas_call(
        halves_kernel,
        out_shape=jax.ShapeDtypeStruct((devices, count // 2, wide), BF16),
        in_specs=[IN_VMEM] + [ANYWHERE] * 3,
        out_specs=IN_VMEM,
        compiler_params=SOME,
        cost_estimate=cost(10**5, 10**5),
        name="halves",
    )(got, chains, own, returned)


def collect(far_col, got, chains, roots, own, returned, count):
    wide = got.shape[2]
    fetched = (far_col, got, chains, roots)
    return pl.pallas_call(
        collect_kernel,
        out_shape=(
            jax.ShapeDtypeStruct((far_col.shape[1], wide), F32),
            jax.ShapeDtypeStruct((count, wide), F32),
            jax.ShapeDtypeStruct((16, chains.shape[1]), F32),
            jax.ShapeDtypeStruct(own.shape, F32),
        ),
        in_specs=[IN_HBM] * 4 + [IN_VMEM] * 2,
        out_specs=(IN_VMEM,) * 4,
        scratch_shapes=[vmem(a) for a in fetched] + [pltpu.SemaphoreType.DMA((4,))],
        compiler_params=MOST,
        cost_estimate=cost(10**7, 3 * 10**6),
        name="collect",
    )(far_col, got, chains, roots, own, returned)


def finish(far_row, far_col, sibling, partner, arrived, down, near, bases, coup):
    count = near.shape[0] // 2
    wide = sibling.shape[2]
    return pl.pallas_call(
        finish_kernel,
        out_shape=jax.ShapeDtypeStruct((count, 2, near.shape[1]), F32),
        in_specs=[IN_VMEM] * 8 + [IN_HBM],
        out_specs=IN_VMEM,
        scratch_shapes=[
            vmem(coup),
            pltpu.VMEM((wide, far_row.shape[1]), F32),
            pltpu.SemaphoreType.DMA((coup.shape[0] // 8,)),
        ],
        compiler_params=pltpu.CompilerParams(vmem_limit_bytes=51 * 1024 * 1024),
        cost_estimate=cost(10**7, 5 * 10**6),
        name="finish",
    )(far_row, far_col, sibling, partner, arrived, down, near, bases, coup)


def shards(
    vectors,
    self_blocks,
    near_blocks,
    near_row,
    near_col,
    bases,
    transfers,
    far_row,
    far_col,
    couplings,
    root_couplings,
):
    count, _, leaf = vectors.shape
    rank = bases.shape[2]
    pairs = far_row.shape[0]
    devices = lax.axis_size(AXES)

    flat_bases = bases.transpose(0, 2, 1).reshape(count * rank, leaf)
    coup = couplings.transpose(1, 2, 0)
    far = (far_row.reshape(1, pairs), far_col.reshape(1, pairs))
    near = (near_row.reshape(1, -1), near_col.reshape(1, -1))
    following = from_behind(vectors, -1)
    payload = pack(devices, *far, vectors, flat_bases, transfers, coup)
    payload, following, x = lax.optimization_barrier((payload, following, vectors))
    got = lax.all_to_all(payload, AXES, 0, 0, tiled=True)
    own, back = near_back(*near, x, near_blocks)
    returned = from_behind(back, 1)
    own = near_main(*near, x, following, own, near_blocks, self_blocks)
    own, late_transfers = lax.optimization_barrier((own, transfers))
    chains = multiply_chains(late_transfers)
    mine = halves(got, chains, own, returned, count)
    sibling = lax.ppermute(mine, AXES, [(i, i ^ 1) for i in range(devices)])
    partner, arrived, down, near_sum = collect(
        far[1], got, chains, root_couplings[0], own, returned, count
    )
    return finish(*far, sibling, partner, arrived, down, near_sum, flat_bases, coup)


def solution(mesh):
    in_specs = (
        P(AXES, None, None),
        P(AXES, None, None),
        P(AXES, None, None),
        P(AXES),
        P(AXES),
        P(AXES, None, None),
        P(AXES, None, None),
        P(AXES),
        P(AXES),
        P(AXES, None, None),
        P(AXES, None, None, None),
    )
    out_specs = P(AXES, None, None)
    return jax.shard_map(shards, mesh=mesh, in_specs=in_specs, out_specs=out_specs, check_vma=False)
```
